32 devices in a mesh: row: 4 (over y, x), col: 4 (over z), layer: 2 (over core).
Axes of the slice: x: 2, y: 2, z: 4, core: 2. Of those that a mesh axis runs over, the one named last changes fastest.
Arguments:
- a_tiles: bfloat16 [4, 2, 4, 16, 128, 128], P('row', 'layer', 'col'), may hold values from -6 to 6
- a_place: int32 [4, 2, 4, 16], P('row', 'layer', 'col'), may hold values from 0 to 31, as said below
- a_count: int32 [4, 2, 4], P('row', 'layer', 'col'), may hold values from 8 to 16, as said below
- b_tiles: bfloat16 [2, 4, 4, 64, 128, 128], P('layer', 'row', 'col'), may hold values from -0.09375 to 0.09375
- b_place: int32 [2, 4, 4, 64], P('layer', 'row', 'col'), may hold values from 0 to 127, as said below
- b_count: int32 [2, 4, 4], P('layer', 'row', 'col'), may hold values from 32 to 64, as said below
- out_place: int32 [4, 4, 32], P('row', 'col'), may hold values from 0 to 63, as said below
Outputs:
- out_tiles: bfloat16 [4, 4, 32, 128, 128], P('row', 'col', 'layer')
The draws below stay inside these ranges and needn't reach their ends.
Inputs may be any that keep to these rules, and one draw needn't show every extreme that they name: `a_place`: the 16 slots of a shard hold distinct positions of its 4 x 8 tile block. `a_count`: some shard uses all its slots. `b_place`: the 64 slots of a shard hold distinct positions of its 8 x 16 tile block. `b_count`: some shard uses all its slots. `out_place`: the 32 positions of a block are distinct positions of its 4 x 16 tile block.
All inputs are finite; a program needn't handle non-finite values.
Results may differ from the reference program's by a relative error of at most 0.001.
Values may be sent and summed in bfloat16 or wider, within the bound.
No kernel may reach another device: no remote copies, remote signals or barrier semaphores. Data moves between devices by JAX's collectives and lax.ppermute only.
A program may use at most 128 MiB of HBM per device.

```python
import jax
import jax.numpy as jnp
from jax import lax

TILE = 128
TB = 4
TBC = 16
KL = 32
KA = 8
KB = 8
NA = 16
NB = 64
NO = 32
N_ROW = 4
N_COL = 4
N_LAYER = 2


def distinct_places(key, leading, span, keep):
    scores = jax.random.randint(key, leading + (span,), 0, 65536) * span + jnp.arange(span, dtype=jnp.int32)
    return jnp.argsort(scores, axis=-1)[..., :keep].astype(jnp.int32)


def ragged_counts(key, leading, most):
    counts = jax.random.randint(key, leading, most // 2, most + 1)
    first = jax.random.randint(jax.random.fold_in(key, 11), (), 0, leading[0])
    second = jax.random.randint(jax.random.fold_in(key, 12), (), 0, leading[1])
    third = jax.random.randint(jax.random.fold_in(key, 13), (), 0, leading[2])
    return counts.at[first, second, third].set(most).astype(jnp.int32)


def draw_a_place(key, part):
    key = jax.random.fold_in(key, 1)
    return distinct_places(key, (N_ROW, N_LAYER, N_COL), TB * KA, NA)


def draw_a_count(key, part):
    key = jax.random.fold_in(key, 2)
    return ragged_counts(key, (N_ROW, N_LAYER, N_COL), NA)


def draw_b_place(key, part):
    key = jax.random.fold_in(key, 3)
    return distinct_places(key, (N_LAYER, N_ROW, N_COL), KB * TBC, NB)


def draw_b_count(key, part):
    key = jax.random.fold_in(key, 4)
    return ragged_counts(key, (N_LAYER, N_ROW, N_COL), NB)


def draw_out_place(key, part):
    key = jax.random.fold_in(key, 5)
    return distinct_places(key, (N_ROW, N_COL), TB * TBC, NO)


def steps_of(rng, dims, pieces, smallest, largest):
    level, own = 1.0, jax.random.fold_in(rng, 6)
    for axis_at, parts in pieces:
        draws = jnp.exp(jax.random.uniform(jax.random.fold_in(own, axis_at), (parts,), jnp.float32, smallest / len(pieces), largest / len(pieces)))
        level = level * jnp.repeat(draws, dims[axis_at] // parts).reshape([-1 if axis == axis_at else 1 for axis in range(len(dims))])
    return level


def scatter_about(key, dims, spread, bound, pieces=(), kind=jnp.bfloat16):
    result = jax.random.normal(key, dims, jnp.float32) * spread
    if len(pieces) > 0:
        result = steps_of(key, dims, pieces, -0.22, 0.18) * result
    return jnp.clip(result, min=-bound, max=bound).astype(kind)


def setup_inputs(seed: int = 0) -> dict:
    key_of = jax.random.split(jax.random.key(seed), 8)
    return {
        "a_tiles": scatter_about(key_of[0], (N_ROW, N_LAYER, N_COL, NA, TILE, TILE), 1.0, 6.0, ((0, 4), (1, 2), (2, 4))),
        "a_place": draw_a_place(jax.random.fold_in(key_of[7], 71), 0),
        "a_count": draw_a_count(jax.random.fold_in(key_of[7], 71), 0),
        "b_tiles": scatter_about(key_of[3], (N_LAYER, N_ROW, N_COL, NB, TILE, TILE), (KL * TILE) ** -0.5, 0.09375, ((0, 2), (1, 4), (2, 4))),
        "b_place": draw_b_place(jax.random.fold_in(key_of[7], 71), 0),
        "b_count": draw_b_count(jax.random.fold_in(key_of[7], 71), 0),
        "out_place": draw_out_place(jax.random.fold_in(key_of[7], 71), 0),
    }


def spread_tiles(tiles, tile_rows, tile_cols, usable, row_count, col_count):
    tile_side = tiles.shape[-1]
    cells_all = row_count * col_count
    flat_index = jnp.where(usable, tile_rows * col_count + tile_cols, cells_all).astype(jnp.int32)
    grid = jnp.zeros((cells_all, tile_side, tile_side), tiles.dtype).at[flat_index].set(tiles, mode="drop")
    grid = grid.reshape(row_count, col_count, tile_side, tile_side).transpose(0, 2, 1, 3)
    return grid.reshape(row_count * tile_side, col_count * tile_side)


def reference(a_tiles, a_place, a_count, b_tiles, b_place, b_count, out_place):
    tile_side = a_tiles.shape[-1]
    span_a = KL // N_COL
    span_b = KL // N_ROW
    row_ids = jnp.arange(N_ROW, dtype=jnp.int32)[:, None, None, None]
    layer_ids = jnp.arange(N_LAYER, dtype=jnp.int32)[None, :, None, None]
    col_ids = jnp.arange(N_COL, dtype=jnp.int32)[None, None, :, None]
    slot_a = jnp.arange(NA, dtype=jnp.int32)[None, None, None, :]
    a_row = row_ids * TB + a_place // span_a
    a_inner = layer_ids * KL + col_ids * span_a + a_place % span_a
    a_usable = slot_a < a_count[..., None]
    a_dense = spread_tiles(a_tiles.reshape(-1, tile_side, tile_side), a_row.reshape(-1), a_inner.reshape(-1),
                           a_usable.reshape(-1), N_ROW * TB, N_LAYER * KL)
    layer_b = jnp.arange(N_LAYER, dtype=jnp.int32)[:, None, None, None]
    row_b = jnp.arange(N_ROW, dtype=jnp.int32)[None, :, None, None]
    col_b = jnp.arange(N_COL, dtype=jnp.int32)[None, None, :, None]
    slot_b = jnp.arange(NB, dtype=jnp.int32)[None, None, None, :]
    b_inner = layer_b * KL + row_b * span_b + b_place // TBC
    b_col = col_b * TBC + b_place % TBC
    b_usable = slot_b < b_count[..., None]
    b_dense = spread_tiles(b_tiles.reshape(-1, tile_side, tile_side), b_inner.reshape(-1), b_col.reshape(-1),
                           b_usable.reshape(-1), N_LAYER * KL, N_COL * TBC)

    def per_block(inputs):
        a_block, places = inputs
        product = jnp.dot(a_block, b_dense, preferred_element_type=jnp.float32)
        grid = product.reshape(TB, tile_side, N_COL, TBC, tile_side).transpose(2, 0, 3, 1, 4)
        grid = grid.reshape(N_COL, TB * TBC, tile_side, tile_side)
        picked = jnp.take_along_axis(grid, places[:, :, None, None].astype(jnp.int32), axis=1)
        return picked.astype(jnp.bfloat16)

    return lax.map(per_block, (a_dense.reshape(N_ROW, TB * tile_side, N_LAYER * KL * tile_side), out_place))
```

```python
import jax
import jax.numpy as jnp
from jax import lax
from jax.experimental import pallas as pl
from jax.experimental.pallas import tpu as pltpu
from jax.sharding import PartitionSpec as P

TB = 4
TBC = 16
KL = 32
WIDE = 4


def place_tiles(tiles, cell, usable, cells_all):
    target = jnp.where(usable, cell, -1).astype(jnp.int32)
    select = (target[:, None] == jnp.arange(cells_all, dtype=jnp.int32)[None, :]).astype(
        tiles.dtype
    )
    placed = jnp.einsum("sc,sab->cab", select, tiles, preferred_element_type=jnp.float32)
    return placed.astype(tiles.dtype)


def unpack_list(tiles, place, count):
    tile_side = tiles.shape[-1]
    slot_count = tiles.shape[3]
    flat_tiles = tiles.reshape(-1, tile_side, tile_side)
    flat_place = place.reshape(-1)
    shard_of = jnp.arange(flat_place.shape[0], dtype=jnp.int32) // slot_count
    slot_of = jnp.arange(flat_place.shape[0], dtype=jnp.int32) % slot_count
    usable = slot_of < jnp.repeat(count.reshape(-1), slot_count)
    return (flat_tiles, flat_place, shard_of, usable)


def tile_product(left_grid, right_grid):
    return jnp.einsum("ikab,kjbc->iajc", left_grid, right_grid, preferred_element_type=jnp.float32)


def gathered_shards(a_tiles, a_place, a_count, b_tiles, b_place, b_count, out_place):
    tile_side = a_tiles.shape[-1]
    span_a = KL // lax.axis_size("col")
    span_b = KL // lax.axis_size("row")
    b_whole = (
        lax.all_gather(b_tiles, "row", axis=1, tiled=True),
        lax.all_gather(b_place, "row", axis=1, tiled=True),
        lax.all_gather(b_count, "row", axis=1, tiled=True),
    )
    b_flat, b_where, b_shard, b_usable = unpack_list(b_whole[0], b_whole[1], b_whole[2])
    b_cell = (b_shard * span_b + b_where // TBC) * TBC + b_where % TBC
    b_grid = place_tiles(b_flat, b_cell, b_usable, KL * TBC).reshape(KL, TBC, tile_side, tile_side)
    piece = (
        lax.all_gather(a_tiles, "col", axis=2, tiled=True),
        lax.all_gather(a_place, "col", axis=2, tiled=True),
        lax.all_gather(a_count, "col", axis=2, tiled=True),
    )
    width = piece[0].shape[2] * span_a
    a_flat, a_where, a_shard, a_usable = unpack_list(piece[0], piece[1], piece[2])
    a_cell = a_where // span_a * width + a_shard * span_a + a_where % span_a
    a_grid = place_tiles(a_flat, a_cell, a_usable, TB * width).reshape(
        TB, width, tile_side, tile_side
    )
    partial_sum = tile_product(a_grid, b_grid)
    pattern = out_place.reshape(-1)
    half_count = pattern.shape[0] // lax.axis_size("layer")
    summed = lax.psum(partial_sum, "layer")
    owned = lax.dynamic_slice_in_dim(pattern, lax.axis_index("layer") * half_count, half_count)
    result = summed[owned // TBC, :, owned % TBC, :]
    return result.astype(jnp.bfloat16).reshape(1, 1, half_count, tile_side, tile_side)


def across(x, axes, pairs):
    return lax.ppermute(x, axes, pairs)


def flip(x, bits):
    return across(x, "row", [(i, i ^ bits) for i in range(4)])


def swap_layers(x):
    return across(x, "layer", [(0, 1), (1, 0)])


def slot_table(place, count, cells):
    slots = place.shape[-1]
    slot = jnp.arange(slots, dtype=jnp.int32)
    hit = (place[:, :, None] == jnp.arange(cells, dtype=jnp.int32)) & (
        slot[None, :, None] < count[:, None, None]
    )
    return slots - jnp.sum(jnp.where(hit, slots - slot[None, :, None], 0), axis=1)


def rows_of(left, table, entry, tiles, span):
    height, side = tiles.shape[-2:]
    for i in range(TB):
        for k in range(span):
            left[i * height : (i + 1) * height, k * side : (k + 1) * side] = tiles[
                table[entry, i * span + k]
            ]


def block_of(left, table, entry, tiles, span, first):
    right = jnp.concatenate(
        [
            jnp.concatenate([tiles[table[entry, k * TBC + first + j]] for j in range(WIDE)], axis=1)
            for k in range(span)
        ],
        axis=0,
    )
    return jnp.dot(left[...], right, preferred_element_type=jnp.float32)


def put_block(grid, first, value):
    side = grid.shape[-1]
    for j in range(WIDE):
        grid[first + j] = value[:, j * side : (j + 1) * side]


def pick(out, grid, table, entry, first):
    height = out.shape[-2]

    def one(o, carry):
        place = table[entry, first + o]
        out[o] = grid[place % TBC, pl.ds(pl.multiple_of((place // TBC) * height, height), height), :]
        return carry

    lax.fori_loop(0, out.shape[0], one, 0, unroll=True)


def note_tile(dtype, height, side, *numbers):
    note = jnp.concatenate([n.reshape(-1) for n in numbers])
    note = jnp.pad(note, (0, side - note.size)).astype(dtype)
    return jnp.broadcast_to(note, (1, height, side))


def note_of(tiles, at):
    return tiles[at, 0].astype(jnp.int32)


def planned_shards(a_tiles, a_place, a_count, b_tiles, b_place, b_count, out_place):
    side = a_tiles.shape[-1]
    na, nb, no = a_place.shape[-1], b_place.shape[-1], out_place.shape[-1]
    row, col, layer = (lax.axis_index(n).astype(jnp.int32) for n in ("row", "col", "layer"))
    span, half, low = KL // 4, no // 2, side // 2
    inner = span * side

    b = b_tiles.reshape(nb, side, side)
    b_x, b_y = flip(b, 1), flip(b, 2)
    a = a_tiles.reshape(na, side, side)
    a = jnp.concatenate(
        [a, jnp.zeros((1, side, side), a.dtype), note_tile(a.dtype, side, side, a_place, a_count)]
    )
    two = across(a, "col", [(c, c ^ 2) for c in range(4)])
    one, three = (across(g, "col", [(c, c ^ 1) for c in range(4)]) for g in (a, two))
    a_got, b_x, b_y = lax.optimization_barrier(([a, one, two, three], b_x, b_y))
    spare = lax.select_n(col ^ row ^ 3, *a_got)
    b_note = note_tile(b.dtype, low, side, b_place, b_count, out_place)
    upper, lower = (jnp.concatenate([g, b_note]) for g in (spare[:, :low], spare[:, low:]))
    upper, lower = flip(upper, 1), flip(lower, 2)
    upper, lower, b_x, b_y, a_got = lax.optimization_barrier((upper, lower, b_x, b_y, a_got))

    a_notes = jnp.stack([note_of(g, na + 1) for g in a_got])
    lefts = jnp.stack(
        [lax.dynamic_index_in_dim(a_notes, col ^ row ^ q, keepdims=False) for q in range(3)]
        + [note_of(upper, na + 1), note_of(lower, na + 1)]
    )
    left_table = slot_table(lefts[:, :na], lefts[:, na], TB * span)
    rights = jnp.stack([note_of(g, -1) for g in (b_note, upper, lower)])
    right_table = slot_table(rights[:, :nb], rights[:, nb], span * TBC)
    places = rights[:, nb + 1 : nb + 1 + no]
    table = jnp.concatenate(
        [
            jnp.pad(left_table, ((0, 0), (0, side - TB * span))),
            right_table,
            jnp.pad(places, ((0, 0), (0, side - no))),
            jnp.pad(jnp.stack([row, col, layer]), (0, side - 3))[None],
        ]
    )

    at_right, at_place, at_where = 5, 8, 11

    def load_rights(refs, tiles, sems):
        copies = [
            pltpu.make_async_copy(ref, tiles.at[n, 0:nb], sems.at[n]) for n, ref in enumerate(refs)
        ]
        for n, c in enumerate(copies):
            c.start()
            tiles[n, nb] = jnp.zeros((side, side), tiles.dtype)
        return copies

    def help_neighbours(table, upper, lower, b_y, b_x, keep, give, left, total, tiles, sems):
        copies = load_rights((b_y, b_x), tiles, sems)
        layer = table[at_where, 2]
        for q, shard in enumerate((upper, lower)):
            rows_of(left.at[q], table, 3 + q, shard, span)
        for q in range(2):
            copies[q].wait()
            for first in range(0, TBC, WIDE):
                part = block_of(left.at[q], table, at_right + 2 - q, tiles.at[q], span, first)
                put_block(total.at[q], first, part)
        for q in range(2):
            pick(give.at[q], total.at[q], table, at_place + 1 + q, (1 - layer) * half)
            pick(keep.at[q], total.at[q], table, at_place + 1 + q, layer * half)

    def own_rows(table, *refs):
        lefts, rights = refs[0:4], refs[4:7]
        keep, give, left, total, tiles, sems = refs[7:]
        copies = load_rights(rights, tiles, sems)
        row, col, layer = (table[at_where, n] for n in range(3))
        for e in range(4):
            q = e ^ col ^ row

            @pl.when(q < 3)
            def _():
                rows_of(left.at[q], table, q, lefts[e], span)

        for c in copies:
            c.wait()
        for first in range(0, TBC, WIDE):
            acc = block_of(left.at[0], table, at_right, tiles.at[0], span, first)
            for q in (1, 2):
                acc = acc + block_of(left.at[q], table, at_right + q, tiles.at[q], span, first)
            put_block(total, first, acc)
        pick(give, total, table, at_place, (1 - layer) * half)
        pick(keep, total, table, at_place, layer * half)

    smem = pl.BlockSpec(memory_space=pltpu.SMEM)
    vmem = pl.BlockSpec(memory_space=pltpu.VMEM)
    hbm = pl.BlockSpec(memory_space=pltpu.HBM)

    def call(kernel, lefts, rights, out, left_blocks, height, grids):
        return pl.pallas_call(
            kernel,
            in_specs=[smem] + [vmem] * len(lefts) + [hbm] * len(rights),
            out_specs=(vmem, vmem),
            out_shape=(out, out),
            scratch_shapes=[
                pltpu.VMEM((left_blocks, TB * height, inner), a.dtype),
                pltpu.VMEM(grids + (TBC, TB * height, side), jnp.float32),
                pltpu.VMEM((len(rights), nb + 1, side, side), b.dtype),
                pltpu.SemaphoreType.DMA((len(rights),)),
            ],
            compiler_params=pltpu.CompilerParams(vmem_limit_bytes=24 * 2**20),
            cost_estimate=pl.CostEstimate(
                flops=2 * left_blocks * TB * height * inner * TBC * side,
                bytes_accessed=sum(g.size for g in (*lefts, *rights)) * 2,
                transcendentals=0,
            ),
            name=kernel.__name__,
        )(table, *lefts, *rights)

    part_keep, part_give = call(
        help_neighbours,
        (upper, lower),
        (b_y, b_x),
        jax.ShapeDtypeStruct((2, half, low, side), jnp.float32),
        2,
        low,
        (2,),
    )
    part_sum = part_keep + swap_layers(part_give)
    part_sum, b_x, b_y, a_got = lax.optimization_barrier((part_sum, b_x, b_y, a_got))
    from_x, from_y = flip(part_sum[0], 1), flip(part_sum[1], 2)
    keep, give = call(
        own_rows,
        a_got,
        (b, b_x, b_y),
        jax.ShapeDtypeStruct((half, side, side), jnp.float32),
        3,
        side,
        (),
    )
    give, from_x, from_y = lax.optimization_barrier((give, from_x, from_y))
    mine = keep + swap_layers(give)
    result = jnp.concatenate([mine[:, :low] + from_x, mine[:, low:] + from_y], axis=1)
    return result.astype(jnp.bfloat16).reshape(1, 1, half, side, side)


def solution(mesh):
    if mesh.shape["row"] == 4 and mesh.shape["col"] == 4:
        body = planned_shards
    else:
        body = gathered_shards
    return jax.shard_map(
        body,
        mesh=mesh,
        in_specs=(
            P("row", "layer", "col", None, None, None),
            P("row", "layer", "col", None),
            P("row", "layer", "col"),
            P("layer", "row", "col", None, None, None),
            P("layer", "row", "col", None),
            P("layer", "row", "col"),
            P("row", "col", None),
        ),
        out_specs=P("row", "col", "layer", None, None),
        check_vma=False,
    )
```

```python
import jax
import jax.numpy as jnp
from jax import lax
from jax.experimental import pallas as pl
from jax.experimental.pallas import tpu as pltpu
from jax.sharding import PartitionSpec as P

TB = 4
TBC = 16
KL = 32
WIDE = 4


def place_tiles(tiles, cell, usable, cells_all):
    target = jnp.where(usable, cell, -1).astype(jnp.int32)
    select = (target[:, None] == jnp.arange(cells_all, dtype=jnp.int32)[None, :]).astype(
        tiles.dtype
    )
    placed = jnp.einsum("sc,sab->cab", select, tiles, preferred_element_type=jnp.float32)
    return placed.astype(tiles.dtype)


def unpack_list(tiles, place, count):
    tile_side = tiles.shape[-1]
    slot_count = tiles.shape[3]
    flat_tiles = tiles.reshape(-1, tile_side, tile_side)
    flat_place = place.reshape(-1)
    shard_of = jnp.arange(flat_place.shape[0], dtype=jnp.int32) // slot_count
    slot_of = jnp.arange(flat_place.shape[0], dtype=jnp.int32) % slot_count
    usable = slot_of < jnp.repeat(count.reshape(-1), slot_count)
    return (flat_tiles, flat_place, shard_of, usable)


def tile_product(left_grid, right_grid):
    return jnp.einsum("ikab,kjbc->iajc", left_grid, right_grid, preferred_element_type=jnp.float32)


def gathered_shards(a_tiles, a_place, a_count, b_tiles, b_place, b_count, out_place):
    tile_side = a_tiles.shape[-1]
    span_a = KL // lax.axis_size("col")
    span_b = KL // lax.axis_size("row")
    b_whole = (
        lax.all_gather(b_tiles, "row", axis=1, tiled=True),
        lax.all_gather(b_place, "row", axis=1, tiled=True),
        lax.all_gather(b_count, "row", axis=1, tiled=True),
    )
    b_flat, b_where, b_shard, b_usable = unpack_list(b_whole[0], b_whole[1], b_whole[2])
    b_cell = (b_shard * span_b + b_where // TBC) * TBC + b_where % TBC
    b_grid = place_tiles(b_flat, b_cell, b_usable, KL * TBC).reshape(KL, TBC, tile_side, tile_side)
    piece = (
        lax.all_gather(a_tiles, "col", axis=2, tiled=True),
        lax.all_gather(a_place, "col", axis=2, tiled=True),
        lax.all_gather(a_count, "col", axis=2, tiled=True),
    )
    width = piece[0].shape[2] * span_a
    a_flat, a_where, a_shard, a_usable = unpack_list(piece[0], piece[1], piece[2])
    a_cell = a_where // span_a * width + a_shard * span_a + a_where % span_a
    a_grid = place_tiles(a_flat, a_cell, a_usable, TB * width).reshape(
        TB, width, tile_side, tile_side
    )
    partial_sum = tile_product(a_grid, b_grid)
    pattern = out_place.reshape(-1)
    half_count = pattern.shape[0] // lax.axis_size("layer")
    summed = lax.psum(partial_sum, "layer")
    owned = lax.dynamic_slice_in_dim(pattern, lax.axis_index("layer") * half_count, half_count)
    result = summed[owned // TBC, :, owned % TBC, :]
    return result.astype(jnp.bfloat16).reshape(1, 1, half_count, tile_side, tile_side)


def across(x, axes, pairs):
    return lax.ppermute(x, axes, pairs)


def flip(x, bits):
    return across(x, "row", [(i, i ^ bits) for i in range(4)])


def swap_layers(x):
    return across(x, "layer", [(0, 1), (1, 0)])


def rows_of(left, table, entry, shard, height):
    side = shard.shape[-1]
    span = left.shape[-1] // side
    for i in range(TB):
        for k in range(span):
            slot = table[entry, i * span + k]
            first = pl.multiple_of(jnp.maximum(slot, 0) * height, height)
            tile = shard[pl.ds(first, height), :]
            left[i * height : (i + 1) * height, k * side : (k + 1) * side] = jnp.where(
                slot >= 0, tile, jnp.zeros_like(tile)
            )


def block_of(left, table, entry, tiles, span, first):
    right = jnp.concatenate(
        [
            jnp.concatenate([tiles[table[entry, k * TBC + first + j]] for j in range(WIDE)], axis=1)
            for k in range(span)
        ],
        axis=0,
    )
    return jnp.dot(left[...], right, preferred_element_type=jnp.float32)


def put_block(grid, first, value):
    side = grid.shape[-1]
    for j in range(WIDE):
        grid[first + j] = value[:, j * side : (j + 1) * side]


def pick(out, grid, table, entry, first, before=None):
    height = out.shape[-2]
    for o in range(out.shape[0]):
        place = table[entry, first + o]
        tile = grid[place % TBC, pl.ds(pl.multiple_of((place // TBC) * height, height), height), :]
        out[o] = tile if before is None else tile + before[o]


def slot_table(place, count, cells):
    slot = jnp.arange(place.shape[-1], dtype=jnp.int32)
    hit = (place[:, :, None] == jnp.arange(cells, dtype=jnp.int32)) & (
        slot[None, :, None] < count[:, None, None]
    )
    return jnp.sum(jnp.where(hit, slot[None, :, None] + 1, 0), axis=1) - 1


def note_rows(dtype, side, *numbers):
    note = jnp.concatenate([n.reshape(-1) for n in numbers])
    note = jnp.pad(note, (0, side - note.size)).astype(dtype)
    return jnp.broadcast_to(note, (16, side))


def note_of(shard):
    return shard[-1].astype(jnp.int32)


def widen(rows, side):
    return jnp.pad(rows, ((0, 0), (0, side - rows.shape[-1])))


def planned_shards(a_tiles, a_place, a_count, b_tiles, b_place, b_count, out_place):
    side = a_tiles.shape[-1]
    na, nb, no = a_place.shape[-1], b_place.shape[-1], out_place.shape[-1]
    row, col, layer = (lax.axis_index(n).astype(jnp.int32) for n in ("row", "col", "layer"))
    span, half, low = KL // 4, no // 2, side // 2
    inner = span * side

    b = b_tiles.reshape(nb, side, side)
    b_x, b_y = flip(b, 1), flip(b, 2)
    a_note = note_rows(a_tiles.dtype, side, a_place, a_count)
    a = jnp.concatenate([a_tiles.reshape(na * side, side), a_note])
    cut = na * side // 2
    two = jnp.concatenate(
        [across(g, "col", [(c, c ^ 2) for c in range(4)]) for g in (a[:cut], a[cut:])]
    )
    one = across(a, "col", [(c, c ^ 1) for c in range(4)])
    b_note = jnp.concatenate([b_place.reshape(-1), b_count.reshape(-1), out_place.reshape(-1)])
    b_note_x, b_note_y = flip(b_note, 1), flip(b_note, 2)
    three = jnp.concatenate(
        [across(g, "col", [(c, c ^ 1) for c in range(4)]) for g in (two[:cut], two[cut:])]
    )
    a_got = [a, one, two, three]
    place = widen(jnp.stack([row, col, layer])[None], side)
    a_notes = jnp.stack([note_of(g) for g in a_got])
    lefts = jnp.stack(
        [lax.dynamic_index_in_dim(a_notes, col ^ row ^ q, keepdims=False) for q in range(3)]
    )
    left_table = widen(slot_table(lefts[:, :na], lefts[:, na], TB * span), side)

    def right_tables(notes):
        table = slot_table(notes[:, :nb], notes[:, nb], span * TBC)
        return jnp.where(table < 0, nb, table), widen(notes[:, nb + 1 :], side)


    def load_rights(refs, tiles, sems):
        copies = [
            pltpu.make_async_copy(ref, tiles.at[n, 0:nb], sems.at[n]) for n, ref in enumerate(refs)
        ]
        for n, c in enumerate(copies):
            c.start()
            tiles[n, nb] = jnp.zeros((side, side), tiles.dtype)
        return copies

    def help_neighbours(
        table, b_y, b_x, upper, lower, keep, give, left, total, tiles, sems, shards, shard_sems, note_v, note_s, slots
    ):
        near = [
            pltpu.make_async_copy(ref, shards.at[q], shard_sems.at[q])
            for q, ref in enumerate((upper, lower))
        ]
        for c in near:
            c.start()
        copies = load_rights((b_y, b_x), tiles, sems)
        layer = table[4, 2]
        for q in range(2):
            near[q].wait()
            note = shards[q, na * low :, :].astype(jnp.float32).astype(jnp.int32)
            note_v[q] = note[: note_v.shape[1]]
        noted = pltpu.make_async_copy(note_v, note_s, shard_sems.at[0])
        noted.start()
        noted.wait()
        for q in range(2):
            for cell in range(TB * span):
                slots[q, cell] = -1
            for slot in range(na):

                @pl.when(slot < note_s[q, 0, na])
                def _():
                    slots[q, note_s[q, 0, slot]] = slot

        for q in range(2):
            rows_of(left.at[q], slots, q, shards.at[q], low)
            copies[q].wait()
            for first in range(0, TBC, WIDE):
                part = block_of(left.at[q], table, q, tiles.at[q], span, first)
                put_block(total.at[q], first, part)
        for q in range(2):
            pick(give.at[q], total.at[q], table, 2 + q, (1 - layer) * half)
            pick(keep.at[q], total.at[q], table, 2 + q, layer * half)

    def own_blocks(blocks):
        def kernel(table, *refs):
            lefts, refs = refs[0:4], refs[4:]
            before, refs = refs[: 2 * (len(blocks) == 2)], refs[2 * (len(blocks) == 2) :]
            rights, refs = refs[: len(blocks)], refs[len(blocks) :]
            keep, give, left, total, tiles, sems = refs
            copies = load_rights(rights, tiles, sems)
            at = 2 * len(blocks) + 1
            row, col, layer = (table[at, n] for n in range(3))
            for e in range(4):
                for n, q in enumerate(blocks):

                    @pl.when((e ^ col ^ row) == q)
                    def _():
                        rows_of(left.at[n], table, n, lefts[e], side)

            for c in copies:
                c.wait()
            for first in range(0, TBC, WIDE):
                acc = None
                for n in range(len(blocks)):
                    part = block_of(left.at[n], table, len(blocks) + n, tiles.at[n], span, first)
                    acc = part if acc is None else acc + part
                put_block(total, first, acc)
            pick(give, total, table, at - 1, (1 - layer) * half, before[1] if before else None)
            pick(keep, total, table, at - 1, layer * half, before[0] if before else None)

        return kernel

    smem = pl.BlockSpec(memory_space=pltpu.SMEM)
    vmem = pl.BlockSpec(memory_space=pltpu.VMEM)
    hbm = pl.BlockSpec(memory_space=pltpu.HBM)

    def call(kernel, name, table, near, rights, out, height, grids, far=()):
        return pl.pallas_call(
            kernel,
            in_specs=[smem] + [vmem] * len(near) + [hbm] * len((*rights, *far)),
            out_specs=(vmem, vmem),
            out_shape=(out, out),
            scratch_shapes=[
                pltpu.VMEM((len(rights), TB * height, inner), a.dtype),
                pltpu.VMEM(grids + (TBC, TB * height, side), jnp.float32),
                pltpu.VMEM((len(rights), nb + 1, side, side), b.dtype),
                pltpu.SemaphoreType.DMA((len(rights),)),
            ]
            + [pltpu.VMEM((len(far), *g.shape), g.dtype) for g in far[:1]]
            + [pltpu.SemaphoreType.DMA((len(far),)) for g in far[:1]]
            + [pltpu.VMEM((len(far), 8, side), jnp.int32) for g in far[:1]]
            + [pltpu.SMEM((len(far), 8, side), jnp.int32) for g in far[:1]]
            + [pltpu.SMEM((len(far), TB * span), jnp.int32) for g in far[:1]],
            compiler_params=pltpu.CompilerParams(vmem_limit_bytes=2**21
                + 2 * len(rights) * (TB * height * inner + (nb + 1) * side * side)
                + 4 * TBC * TB * height * side * max(1, len(grids) * 2)),
            cost_estimate=pl.CostEstimate(
                flops=2 * len(rights) * TB * height * inner * TBC * side,
                bytes_accessed=sum(g.size for g in rights) * 2,
                transcendentals=0,
            ),
            name=name,
        )(table, *near, *rights, *far)

    whole = jax.ShapeDtypeStruct((half, side, side), jnp.float32)
    spare = lax.select_n(col ^ row ^ 3, *a_got)
    tiles = spare[: na * side].reshape(na, side, side)
    upper, lower = (
        jnp.concatenate([g.reshape(na * low, side), spare[na * side :]])
        for g in (tiles[:, :low], tiles[:, low:])
    )
    upper, lower = flip(upper, 1), flip(lower, 2)

    own_table, pattern = right_tables(b_note[None])
    own_table = jnp.concatenate([left_table[:1], own_table, pattern, place])
    keep, give = call(own_blocks((0,)), "own_block", own_table, a_got, (b,), whole, side, ())
    a_got, b_x, b_y, b_note_x, b_note_y, keep, give = lax.optimization_barrier(
        (a_got, b_x, b_y, b_note_x, b_note_y, keep, give)
    )
    right_table, patterns = right_tables(jnp.stack([b_note_x, b_note_y]))
    table = jnp.concatenate([left_table[1:], right_table, pattern, place])
    keep, give = call(
        own_blocks((1, 2)), "near_blocks", table, (*a_got, keep, give), (b_x, b_y), whole, side, ()
    )
    upper, lower, keep, give = lax.optimization_barrier((upper, lower, keep, give))
    table = jnp.concatenate([right_table[1:], right_table[:1], patterns, place])
    part = jax.ShapeDtypeStruct((2, half, low, side), jnp.float32)
    part_keep, part_give = call(
        help_neighbours, "help_neighbours", table, (), (b_y, b_x), part, low, (2,), (upper, lower)
    )
    part_other = swap_layers(part_give)
    other = swap_layers(give)
    steps = half * low

    def encode(keep, other, *codes):
        for q, code in enumerate(codes):
            values = [keep[q, o] + other[q, o] for o in range(half)]
            tops = [jnp.max(jnp.abs(v), axis=0, keepdims=True) for v in values]
            top = jnp.maximum(jnp.concatenate(tops, axis=0), 1e-30)
            exponent = jnp.ceil(jnp.log2(top))
            scale = jnp.exp2(15.0 - exponent)
            for o, value in enumerate(values):
                value = jnp.clip(value * scale[o : o + 1, :], -32767.0, 32767.0)
                value = jnp.round(value).astype(jnp.int32)
                code[o * low : (o + 1) * low, :] = value.astype(jnp.int16)
            code[steps:, :] = exponent.astype(jnp.int32).astype(jnp.int16)

    def finish(keep, other, from_x, from_y, out):
        for q, code in enumerate((from_x, from_y)):
            step = jnp.exp2(code[steps:, :].astype(jnp.int32).astype(jnp.float32) - 15.0)
            for o in range(half):
                at = (o, slice(q * low, (q + 1) * low), slice(None))
                part = code[o * low : (o + 1) * low, :].astype(jnp.int32).astype(jnp.float32)
                out[at] = (keep[at] + other[at] + part * step[o : o + 1, :]).astype(out.dtype)

    code = jax.ShapeDtypeStruct((steps + half, side), jnp.int16)
    code_x, code_y = pl.pallas_call(
        encode, in_specs=[vmem] * 2, out_specs=(vmem, vmem), out_shape=(code, code), name="encode",
        compiler_params=pltpu.CompilerParams(vmem_limit_bytes=4 * 2**20),
    )(part_keep, part_other)
    from_x, from_y = flip(code_x, 1), flip(code_y, 2)
    result = pl.pallas_call(
        finish,
        in_specs=[vmem] * 4,
        out_specs=vmem,
        out_shape=jax.ShapeDtypeStruct((half, side, side), jnp.bfloat16),
        name="finish",
        compiler_params=pltpu.CompilerParams(vmem_limit_bytes=4 * 2**20),
    )(keep, other, from_x, from_y)
    return result.reshape(1, 1, half, side, side)


def solution(mesh):
    if mesh.shape["row"] == 4 and mesh.shape["col"] == 4:
        body = planned_shards
    else:
        body = gathered_shards
    return jax.shard_map(
        body,
        mesh=mesh,
        in_specs=(
            P("row", "layer", "col", None, None, None),
            P("row", "layer", "col", None),
            P("row", "layer", "col"),
            P("layer", "row", "col", None, None, None),
            P("layer", "row", "col", None),
            P("layer", "row", "col"),
            P("row", "col", None),
        ),
        out_specs=P("row", "col", "layer", None, None),
        check_vma=False,
    )
```

```python
import jax
import jax.numpy as jnp
from jax import lax
from jax.experimental import pallas as pl
from jax.experimental.pallas import tpu as pltpu
from jax.sharding import PartitionSpec as P

TB = 4
TBC = 16
KL = 32
WIDE = 4


def place_tiles(tiles, cell, usable, cells_all):
    target = jnp.where(usable, cell, -1).astype(jnp.int32)
    select = (target[:, None] == jnp.arange(cells_all, dtype=jnp.int32)[None, :]).astype(
        tiles.dtype
    )
    placed = jnp.einsum("sc,sab->cab", select, tiles, preferred_element_type=jnp.float32)
    return placed.astype(tiles.dtype)


def unpack_list(tiles, place, count):
    tile_side = tiles.shape[-1]
    slot_count = tiles.shape[3]
    flat_tiles = tiles.reshape(-1, tile_side, tile_side)
    flat_place = place.reshape(-1)
    shard_of = jnp.arange(flat_place.shape[0], dtype=jnp.int32) // slot_count
    slot_of = jnp.arange(flat_place.shape[0], dtype=jnp.int32) % slot_count
    usable = slot_of < jnp.repeat(count.reshape(-1), slot_count)
    return (flat_tiles, flat_place, shard_of, usable)


def tile_product(left_grid, right_grid):
    return jnp.einsum("ikab,kjbc->iajc", left_grid, right_grid, preferred_element_type=jnp.float32)


def gathered_shards(a_tiles, a_place, a_count, b_tiles, b_place, b_count, out_place):
    tile_side = a_tiles.shape[-1]
    span_a = KL // lax.axis_size("col")
    span_b = KL // lax.axis_size("row")
    b_whole = (
        lax.all_gather(b_tiles, "row", axis=1, tiled=True),
        lax.all_gather(b_place, "row", axis=1, tiled=True),
        lax.all_gather(b_count, "row", axis=1, tiled=True),
    )
    b_flat, b_where, b_shard, b_usable = unpack_list(b_whole[0], b_whole[1], b_whole[2])
    b_cell = (b_shard * span_b + b_where // TBC) * TBC + b_where % TBC
    b_grid = place_tiles(b_flat, b_cell, b_usable, KL * TBC).reshape(KL, TBC, tile_side, tile_side)
    piece = (
        lax.all_gather(a_tiles, "col", axis=2, tiled=True),
        lax.all_gather(a_place, "col", axis=2, tiled=True),
        lax.all_gather(a_count, "col", axis=2, tiled=True),
    )
    width = piece[0].shape[2] * span_a
    a_flat, a_where, a_shard, a_usable = unpack_list(piece[0], piece[1], piece[2])
    a_cell = a_where // span_a * width + a_shard * span_a + a_where % span_a
    a_grid = place_tiles(a_flat, a_cell, a_usable, TB * width).reshape(
        TB, width, tile_side, tile_side
    )
    partial_sum = tile_product(a_grid, b_grid)
    pattern = out_place.reshape(-1)
    half_count = pattern.shape[0] // lax.axis_size("layer")
    summed = lax.psum(partial_sum, "layer")
    owned = lax.dynamic_slice_in_dim(pattern, lax.axis_index("layer") * half_count, half_count)
    result = summed[owned // TBC, :, owned % TBC, :]
    return result.astype(jnp.bfloat16).reshape(1, 1, half_count, tile_side, tile_side)


def across(x, axes, pairs):
    return lax.ppermute(x, axes, pairs)


def flip(x, bits):
    return across(x, "row", [(i, i ^ bits) for i in range(4)])


def swap_layers(x):
    return across(x, "layer", [(0, 1), (1, 0)])


def rows_of(left, table, entry, shard, height):
    side = shard.shape[-1]
    span = left.shape[-1] // side
    for i in range(TB):
        for k in range(span):
            slot = table[entry, i * span + k]
            first = pl.multiple_of(jnp.maximum(slot, 0) * height, height)
            tile = shard[pl.ds(first, height), :]
            left[i * height : (i + 1) * height, k * side : (k + 1) * side] = jnp.where(
                slot >= 0, tile, jnp.zeros_like(tile)
            )


def block_of(left, table, entry, tiles, span, first):
    right = jnp.concatenate(
        [
            jnp.concatenate([tiles[table[entry, k * TBC + first + j]] for j in range(WIDE)], axis=1)
            for k in range(span)
        ],
        axis=0,
    )
    return jnp.dot(left[...], right, preferred_element_type=jnp.float32)


def put_block(grid, first, value):
    side = grid.shape[-1]
    for j in range(WIDE):
        grid[first + j] = value[:, j * side : (j + 1) * side]


def pick(out, grid, table, entry, first, before=None):
    height = out.shape[-2]
    for o in range(out.shape[0]):
        place = table[entry, first + o]
        tile = grid[place % TBC, pl.ds(pl.multiple_of((place // TBC) * height, height), height), :]
        out[o] = tile if before is None else tile + before[o]


def slot_table(place, count, cells):
    slot = jnp.arange(place.shape[-1], dtype=jnp.int32)
    hit = (place[:, :, None] == jnp.arange(cells, dtype=jnp.int32)) & (
        slot[None, :, None] < count[:, None, None]
    )
    return jnp.sum(jnp.where(hit, slot[None, :, None] + 1, 0), axis=1) - 1


def note_rows(dtype, side, *numbers):
    note = jnp.concatenate([n.reshape(-1) for n in numbers])
    note = jnp.pad(note, (0, side - note.size)).astype(dtype)
    return jnp.broadcast_to(note, (16, side))


def note_of(shard):
    return shard[-1].astype(jnp.int32)


def widen(rows, side):
    return jnp.pad(rows, ((0, 0), (0, side - rows.shape[-1])))


def planned_shards(a_tiles, a_place, a_count, b_tiles, b_place, b_count, out_place):
    side = a_tiles.shape[-1]
    na, nb, no = a_place.shape[-1], b_place.shape[-1], out_place.shape[-1]
    row, col, layer = (lax.axis_index(n).astype(jnp.int32) for n in ("row", "col", "layer"))
    span, half, low = KL // 4, no // 2, side // 2
    inner = span * side

    b = b_tiles.reshape(nb, side, side)
    b_x, b_y = flip(b, 1), flip(b, 2)
    a_note = note_rows(a_tiles.dtype, side, a_place, a_count)
    a = jnp.concatenate([a_tiles.reshape(na * side, side), a_note])
    cut = na * side // 2
    two = [across(g, "col", [(c, c ^ 2) for c in range(4)]) for g in (a[:cut], a[cut:])]
    one = across(a, "col", [(c, c ^ 1) for c in range(4)])
    b_note = jnp.concatenate([b_place.reshape(-1), b_count.reshape(-1), out_place.reshape(-1)])
    b_note_x, b_note_y = flip(b_note, 1), flip(b_note, 2)
    three = [across(g, "col", [(c, c ^ 1) for c in range(4)]) for g in two]
    two, three = jnp.concatenate(two), jnp.concatenate(three)
    a_got = [a, one, two, three]
    place = widen(jnp.stack([row, col, layer])[None], side)
    a_notes = jnp.stack([note_of(g) for g in a_got])
    lefts = jnp.stack(
        [lax.dynamic_index_in_dim(a_notes, col ^ row ^ q, keepdims=False) for q in range(3)]
    )
    left_table = widen(slot_table(lefts[:, :na], lefts[:, na], TB * span), side)

    def right_tables(notes):
        table = slot_table(notes[:, :nb], notes[:, nb], span * TBC)
        return jnp.where(table < 0, nb, table), widen(notes[:, nb + 1 :], side)


    def load_rights(refs, tiles, sems):
        copies = [
            pltpu.make_async_copy(ref, tiles.at[n, 0:nb], sems.at[n]) for n, ref in enumerate(refs)
        ]
        for n, c in enumerate(copies):
            c.start()
            tiles[n, nb] = jnp.zeros((side, side), tiles.dtype)
        return copies

    def help_neighbours(
        table, b_y, b_x, upper, lower, keep, give, left, total, tiles, sems, shards, shard_sems, note_v, note_s, slots
    ):
        near = [
            pltpu.make_async_copy(ref, shards.at[q], shard_sems.at[q])
            for q, ref in enumerate((upper, lower))
        ]
        for c in near:
            c.start()
        copies = load_rights((b_y, b_x), tiles, sems)
        layer = table[4, 2]
        for q in range(2):
            near[q].wait()
            note = shards[q, na * low :, :].astype(jnp.float32).astype(jnp.int32)
            note_v[q] = note[: note_v.shape[1]]
        noted = pltpu.make_async_copy(note_v, note_s, shard_sems.at[0])
        noted.start()
        noted.wait()
        for q in range(2):
            for cell in range(TB * span):
                slots[q, cell] = -1
            for slot in range(na):

                @pl.when(slot < note_s[q, 0, na])
                def _():
                    slots[q, note_s[q, 0, slot]] = slot

        for q in range(2):
            rows_of(left.at[q], slots, q, shards.at[q], low)
            copies[q].wait()
            for first in range(0, TBC, WIDE):
                part = block_of(left.at[q], table, q, tiles.at[q], span, first)
                put_block(total.at[q], first, part)
        for q in range(2):
            pick(give.at[q], total.at[q], table, 2 + q, (1 - layer) * half)
            pick(keep.at[q], total.at[q], table, 2 + q, layer * half)

    def own_blocks(blocks):
        def kernel(table, *refs):
            lefts, refs = refs[0:4], refs[4:]
            before, refs = refs[: 2 * (len(blocks) == 2)], refs[2 * (len(blocks) == 2) :]
            rights, refs = refs[: len(blocks)], refs[len(blocks) :]
            keep, give, left, total, tiles, sems = refs
            copies = load_rights(rights, tiles, sems)
            at = 2 * len(blocks) + 1
            row, col, layer = (table[at, n] for n in range(3))
            for e in range(4):
                for n, q in enumerate(blocks):

                    @pl.when((e ^ col ^ row) == q)
                    def _():
                        rows_of(left.at[n], table, n, lefts[e], side)

            for first in range(0, TBC, WIDE):
                acc = None
                for n in range(len(blocks)):
                    if first == 0:
                        copies[n].wait()
                    part = block_of(left.at[n], table, len(blocks) + n, tiles.at[n], span, first)
                    acc = part if acc is None else acc + part
                put_block(total, first, acc)
            pick(give, total, table, at - 1, (1 - layer) * half, before[1] if before else None)
            pick(keep, total, table, at - 1, layer * half, before[0] if before else None)

        return kernel

    smem = pl.BlockSpec(memory_space=pltpu.SMEM)
    vmem = pl.BlockSpec(memory_space=pltpu.VMEM)
    hbm = pl.BlockSpec(memory_space=pltpu.HBM)

    def call(kernel, name, table, near, rights, out, height, grids, far=()):
        return pl.pallas_call(
            kernel,
            in_specs=[smem] + [vmem] * len(near) + [hbm] * len((*rights, *far)),
            out_specs=(vmem, vmem),
            out_shape=(out, out),
            scratch_shapes=[
                pltpu.VMEM((len(rights), TB * height, inner), a.dtype),
                pltpu.VMEM(grids + (TBC, TB * height, side), jnp.float32),
                pltpu.VMEM((len(rights), nb + 1, side, side), b.dtype),
                pltpu.SemaphoreType.DMA((len(rights),)),
            ]
            + [pltpu.VMEM((len(far), *g.shape), g.dtype) for g in far[:1]]
            + [pltpu.SemaphoreType.DMA((len(far),)) for g in far[:1]]
            + [pltpu.VMEM((len(far), 8, side), jnp.int32) for g in far[:1]]
            + [pltpu.SMEM((len(far), 8, side), jnp.int32) for g in far[:1]]
            + [pltpu.SMEM((len(far), TB * span), jnp.int32) for g in far[:1]],
            compiler_params=pltpu.CompilerParams(vmem_limit_bytes=5 * 2**20
                + 2 * len(rights) * (TB * height * inner + (nb + 1) * side * side)
                + 4 * TBC * TB * height * side * max(1, len(grids) * 2)),
            cost_estimate=pl.CostEstimate(
                flops=2 * len(rights) * TB * height * inner * TBC * side,
                bytes_accessed=sum(g.size for g in rights) * 2,
                transcendentals=0,
            ),
            name=name,
        )(table, *near, *rights, *far)

    whole = jax.ShapeDtypeStruct((half, side, side), jnp.float32)
    spare = lax.select_n(col ^ row ^ 3, *a_got)
    tiles = spare[: na * side].reshape(na, side, side)
    upper, lower = (
        jnp.concatenate([g.reshape(na * low, side), spare[na * side :]])
        for g in (tiles[:, :low], tiles[:, low:])
    )
    upper, lower = flip(upper, 1), flip(lower, 2)

    own_table, pattern = right_tables(b_note[None])
    own_table = jnp.concatenate([left_table[:1], own_table, pattern, place])
    keep, give = call(own_blocks((0,)), "own_block", own_table, a_got, (b,), whole, side, ())
    a_got, b_x, b_y, b_note_x, b_note_y, keep, give = lax.optimization_barrier(
        (a_got, b_x, b_y, b_note_x, b_note_y, keep, give)
    )
    right_table, patterns = right_tables(jnp.stack([b_note_x, b_note_y]))
    table = jnp.concatenate([left_table[1:], right_table, pattern, place])
    keep, give = call(
        own_blocks((1, 2)), "near_blocks", table, (*a_got, keep, give), (b_x, b_y), whole, side, ()
    )
    upper, lower, keep, give = lax.optimization_barrier((upper, lower, keep, give))
    table = jnp.concatenate([right_table[1:], right_table[:1], patterns, place])
    part = jax.ShapeDtypeStruct((2, half, low, side), jnp.float32)
    part_keep, part_give = call(
        help_neighbours, "help_neighbours", table, (), (b_y, b_x), part, low, (2,), (upper, lower)
    )
    part_other = swap_layers(part_give)
    other = swap_layers(give)
    steps = half * low

    def encode(keep, other, *codes):
        for q, code in enumerate(codes):
            values = [keep[q, o] + other[q, o] for o in range(half)]
            tops = [jnp.max(jnp.abs(v), axis=0, keepdims=True) for v in values]
            top = jnp.maximum(jnp.concatenate(tops, axis=0), 1e-30)
            exponent = jnp.ceil(jnp.log2(top))
            scale = jnp.exp2(15.0 - exponent)
            for o, value in enumerate(values):
                value = jnp.clip(value * scale[o : o + 1, :], -32767.0, 32767.0)
                value = jnp.round(value).astype(jnp.int32)
                code[o * low : (o + 1) * low, :] = value.astype(jnp.int16)
            code[steps:, :] = exponent.astype(jnp.int32).astype(jnp.int16)

    def finish(mine, from_x, from_y, out, rounded, sems):
        codes = (from_x, from_y)
        scales = [jnp.exp2(c[steps:, :].astype(jnp.int32).astype(jnp.float32) - 15.0) for c in codes]
        copies = []
        for o in range(half):
            for q in range(2):
                at = (o, slice(q * low, (q + 1) * low), slice(None))
                part = codes[q][o * low : (o + 1) * low, :].astype(jnp.int32).astype(jnp.float32)
                rounded[at] = (mine[at] + part * scales[q][o : o + 1, :]).astype(rounded.dtype)
            if (o + 1) % (half // 4) == 0:
                done = slice(o + 1 - half // 4, o + 1)
                copies.append(
                    pltpu.make_async_copy(rounded.at[done], out.at[done], sems.at[len(copies)])
                )
                copies[-1].start()
        for c in copies:
            c.wait()

    code = jax.ShapeDtypeStruct((steps + half, side), jnp.int16)
    code_x, code_y = pl.pallas_call(
        encode, in_specs=[vmem] * 2, out_specs=(vmem, vmem), out_shape=(code, code), name="encode",
        compiler_params=pltpu.CompilerParams(vmem_limit_bytes=10 * 2**20),
    )(part_keep, part_other)
    from_x, from_y = flip(code_x, 1), flip(code_y, 2)
    mine = keep + other
    result = pl.pallas_call(
        finish,
        in_specs=[vmem] * 3,
        out_specs=hbm,
        out_shape=jax.ShapeDtypeStruct((half, side, side), jnp.bfloat16),
        scratch_shapes=[
            pltpu.VMEM((half, side, side), jnp.bfloat16),
            pltpu.SemaphoreType.DMA((4,)),
        ],
        name="finish",
        compiler_params=pltpu.CompilerParams(vmem_limit_bytes=10 * 2**20),
    )(mine, from_x, from_y)
    return result.reshape(1, 1, half, side, side)


def solution(mesh):
    if mesh.shape["row"] == 4 and mesh.shape["col"] == 4:
        body = planned_shards
    else:
        body = gathered_shards
    return jax.shard_map(
        body,
        mesh=mesh,
        in_specs=(
            P("row", "layer", "col", None, None, None),
            P("row", "layer", "col", None),
            P("row", "layer", "col"),
            P("layer", "row", "col", None, None, None),
            P("layer", "row", "col", None),
            P("layer", "row", "col"),
            P("row", "col", None),
        ),
        out_specs=P("row", "col", "layer", None, None),
        check_vma=False,
    )
```

```python
import jax
import jax.numpy as jnp
from jax import lax
from jax.experimental import pallas as pl
from jax.experimental.pallas import tpu as pltpu
from jax.sharding import PartitionSpec as P

TB = 4
TBC = 16
KL = 32
WIDE = 4


def place_tiles(tiles, cell, usable, cells_all):
    target = jnp.where(usable, cell, -1).astype(jnp.int32)
    select = (target[:, None] == jnp.arange(cells_all, dtype=jnp.int32)[None, :]).astype(
        tiles.dtype
    )
    placed = jnp.einsum("sc,sab->cab", select, tiles, preferred_element_type=jnp.float32)
    return placed.astype(tiles.dtype)


def unpack_list(tiles, place, count):
    tile_side = tiles.shape[-1]
    slot_count = tiles.shape[3]
    flat_tiles = tiles.reshape(-1, tile_side, tile_side)
    flat_place = place.reshape(-1)
    shard_of = jnp.arange(flat_place.shape[0], dtype=jnp.int32) // slot_count
    slot_of = jnp.arange(flat_place.shape[0], dtype=jnp.int32) % slot_count
    usable = slot_of < jnp.repeat(count.reshape(-1), slot_count)
    return (flat_tiles, flat_place, shard_of, usable)


def tile_product(left_grid, right_grid):
    return jnp.einsum("ikab,kjbc->iajc", left_grid, right_grid, preferred_element_type=jnp.float32)


def gathered_shards(a_tiles, a_place, a_count, b_tiles, b_place, b_count, out_place):
    tile_side = a_tiles.shape[-1]
    span_a = KL // lax.axis_size("col")
    span_b = KL // lax.axis_size("row")
    b_whole = (
        lax.all_gather(b_tiles, "row", axis=1, tiled=True),
        lax.all_gather(b_place, "row", axis=1, tiled=True),
        lax.all_gather(b_count, "row", axis=1, tiled=True),
    )
    b_flat, b_where, b_shard, b_usable = unpack_list(b_whole[0], b_whole[1], b_whole[2])
    b_cell = (b_shard * span_b + b_where // TBC) * TBC + b_where % TBC
    b_grid = place_tiles(b_flat, b_cell, b_usable, KL * TBC).reshape(KL, TBC, tile_side, tile_side)
    piece = (
        lax.all_gather(a_tiles, "col", axis=2, tiled=True),
        lax.all_gather(a_place, "col", axis=2, tiled=True),
        lax.all_gather(a_count, "col", axis=2, tiled=True),
    )
    width = piece[0].shape[2] * span_a
    a_flat, a_where, a_shard, a_usable = unpack_list(piece[0], piece[1], piece[2])
    a_cell = a_where // span_a * width + a_shard * span_a + a_where % span_a
    a_grid = place_tiles(a_flat, a_cell, a_usable, TB * width).reshape(
        TB, width, tile_side, tile_side
    )
    partial_sum = tile_product(a_grid, b_grid)
    pattern = out_place.reshape(-1)
    half_count = pattern.shape[0] // lax.axis_size("layer")
    summed = lax.psum(partial_sum, "layer")
    owned = lax.dynamic_slice_in_dim(pattern, lax.axis_index("layer") * half_count, half_count)
    result = summed[owned // TBC, :, owned % TBC, :]
    return result.astype(jnp.bfloat16).reshape(1, 1, half_count, tile_side, tile_side)


def across(x, axes, pairs):
    return lax.ppermute(x, axes, pairs)


def flip(x, bits):
    return across(x, "row", [(i, i ^ bits) for i in range(4)])


def swap_layers(x):
    return across(x, "layer", [(0, 1), (1, 0)])


def rows_of(left, table, entry, shard, height):
    side = shard.shape[-1]
    span = left.shape[-1] // side
    for i in range(TB):
        for k in range(span):
            slot = table[entry, i * span + k]
            first = pl.multiple_of(jnp.maximum(slot, 0) * height, height)
            tile = shard[pl.ds(first, height), :]
            left[i * height : (i + 1) * height, k * side : (k + 1) * side] = jnp.where(
                slot >= 0, tile, jnp.zeros_like(tile)
            )


def block_of(left, table, entry, tiles, span, first):
    right = jnp.concatenate(
        [
            jnp.concatenate([tiles[table[entry, k * TBC + first + j]] for j in range(WIDE)], axis=1)
            for k in range(span)
        ],
        axis=0,
    )
    return jnp.dot(left[...], right, preferred_element_type=jnp.float32)


def put_block(grid, first, value):
    side = grid.shape[-1]
    for j in range(WIDE):
        grid[first + j] = value[:, j * side : (j + 1) * side]


def pick(out, grid, table, entry, first, before=None):
    height = out.shape[-2]
    for o in range(out.shape[0]):
        place = table[entry, first + o]
        tile = grid[place % TBC, pl.ds(pl.multiple_of((place // TBC) * height, height), height), :]
        out[o] = tile if before is None else tile + before[o]


def slot_table(place, count, cells):
    slot = jnp.arange(place.shape[-1], dtype=jnp.int32)
    hit = (place[:, :, None] == jnp.arange(cells, dtype=jnp.int32)) & (
        slot[None, :, None] < count[:, None, None]
    )
    return jnp.sum(jnp.where(hit, slot[None, :, None] + 1, 0), axis=1) - 1


def note_rows(dtype, side, *numbers):
    note = jnp.concatenate([n.reshape(-1) for n in numbers])
    note = jnp.pad(note, (0, side - note.size)).astype(dtype)
    return jnp.broadcast_to(note, (16, side))


def note_of(shard):
    return shard[-1].astype(jnp.int32)


def widen(rows, side):
    return jnp.pad(rows, ((0, 0), (0, side - rows.shape[-1])))


def planned_shards(a_tiles, a_place, a_count, b_tiles, b_place, b_count, out_place):
    side = a_tiles.shape[-1]
    na, nb, no = a_place.shape[-1], b_place.shape[-1], out_place.shape[-1]
    row, col, layer = (lax.axis_index(n).astype(jnp.int32) for n in ("row", "col", "layer"))
    span, half, low = KL // 4, no // 2, side // 2
    inner = span * side

    b = b_tiles.reshape(nb, side, side)
    b_x, b_y = flip(b, 1), flip(b, 2)
    a_note = note_rows(a_tiles.dtype, side, a_place, a_count)
    a = jnp.concatenate([a_tiles.reshape(na * side, side), a_note])
    cut = na * side // 2
    two = [across(g, "col", [(c, c ^ 2) for c in range(4)]) for g in (a[:cut], a[cut:])]
    one = across(a, "col", [(c, c ^ 1) for c in range(4)])
    b_note = jnp.concatenate([b_place.reshape(-1), b_count.reshape(-1), out_place.reshape(-1)])
    b_note_x, b_note_y = flip(b_note, 1), flip(b_note, 2)
    three = [across(g, "col", [(c, c ^ 1) for c in range(4)]) for g in two]
    two, three = jnp.concatenate(two), jnp.concatenate(three)
    a_got = [a, one, two, three]
    place = widen(jnp.stack([row, col, layer])[None], side)
    a_notes = jnp.stack([note_of(g) for g in a_got])
    lefts = jnp.stack(
        [lax.dynamic_index_in_dim(a_notes, col ^ row ^ q, keepdims=False) for q in range(3)]
    )
    left_table = widen(slot_table(lefts[:, :na], lefts[:, na], TB * span), side)

    def right_tables(notes):
        table = slot_table(notes[:, :nb], notes[:, nb], span * TBC)
        return jnp.where(table < 0, nb, table), widen(notes[:, nb + 1 :], side)


    def load_rights(refs, tiles, sems):
        copies = [
            pltpu.make_async_copy(ref, tiles.at[n, 0:nb], sems.at[n]) for n, ref in enumerate(refs)
        ]
        for n, c in enumerate(copies):
            c.start()
            tiles[n, nb] = jnp.zeros((side, side), tiles.dtype)
        return copies

    def help_neighbours(
        table, b_y, b_x, upper, lower, keep, give, left, total, tiles, sems, shards, shard_sems, note_v, note_s, slots
    ):
        near = [
            pltpu.make_async_copy(ref, shards.at[q], shard_sems.at[q])
            for q, ref in enumerate((upper, lower))
        ]
        for c in near:
            c.start()
        copies = load_rights((b_y, b_x), tiles, sems)
        layer = table[4, 2]
        for q in range(2):
            near[q].wait()
            note = shards[q, na * low :, :].astype(jnp.float32).astype(jnp.int32)
            note_v[q] = note[: note_v.shape[1]]
        noted = pltpu.make_async_copy(note_v, note_s, shard_sems.at[0])
        noted.start()
        noted.wait()
        for q in range(2):
            for cell in range(TB * span):
                slots[q, cell] = -1
            for slot in range(na):

                @pl.when(slot < note_s[q, 0, na])
                def _():
                    slots[q, note_s[q, 0, slot]] = slot

        for q in range(2):
            rows_of(left.at[q], slots, q, shards.at[q], low)
            copies[q].wait()
            for first in range(0, TBC, WIDE):
                part = block_of(left.at[q], table, q, tiles.at[q], span, first)
                put_block(total.at[q], first, part)
        for q in range(2):
            pick(give.at[q], total.at[q], table, 2 + q, (1 - layer) * half)
            pick(keep.at[q], total.at[q], table, 2 + q, layer * half)

    def own_blocks(blocks):
        def kernel(table, *refs):
            lefts, refs = refs[0:4], refs[4:]
            before, refs = refs[: 2 * (len(blocks) == 2)], refs[2 * (len(blocks) == 2) :]
            rights, refs = refs[: len(blocks)], refs[len(blocks) :]
            keep, give, left, total, tiles, sems = refs
            copies = load_rights(rights, tiles, sems)
            at = 2 * len(blocks) + 1
            row, col, layer = (table[at, n] for n in range(3))
            for e in range(4):
                for n, q in enumerate(blocks):

                    @pl.when((e ^ col ^ row) == q)
                    def _():
                        rows_of(left.at[n], table, n, lefts[e], side)

            for first in range(0, TBC, WIDE):
                acc = None
                for n in range(len(blocks)):
                    if first == 0:
                        copies[n].wait()
                    part = block_of(left.at[n], table, len(blocks) + n, tiles.at[n], span, first)
                    acc = part if acc is None else acc + part
                put_block(total, first, acc)
            pick(give, total, table, at - 1, (1 - layer) * half, before[1] if before else None)
            pick(keep, total, table, at - 1, layer * half, before[0] if before else None)

        return kernel

    smem = pl.BlockSpec(memory_space=pltpu.SMEM)
    vmem = pl.BlockSpec(memory_space=pltpu.VMEM)
    hbm = pl.BlockSpec(memory_space=pltpu.HBM)

    def call(kernel, name, table, near, rights, out, height, grids, far=()):
        return pl.pallas_call(
            kernel,
            in_specs=[smem] + [vmem] * len(near) + [hbm] * len((*rights, *far)),
            out_specs=(vmem, vmem),
            out_shape=(out, out),
            scratch_shapes=[
                pltpu.VMEM((len(rights), TB * height, inner), a.dtype),
                pltpu.VMEM(grids + (TBC, TB * height, side), jnp.float32),
                pltpu.VMEM((len(rights), nb + 1, side, side), b.dtype),
                pltpu.SemaphoreType.DMA((len(rights),)),
            ]
            + [pltpu.VMEM((len(far), *g.shape), g.dtype) for g in far[:1]]
            + [pltpu.SemaphoreType.DMA((len(far),)) for g in far[:1]]
            + [pltpu.VMEM((len(far), 8, side), jnp.int32) for g in far[:1]]
            + [pltpu.SMEM((len(far), 8, side), jnp.int32) for g in far[:1]]
            + [pltpu.SMEM((len(far), TB * span), jnp.int32) for g in far[:1]],
            compiler_params=pltpu.CompilerParams(vmem_limit_bytes=5 * 2**20
                + 2 * len(rights) * (TB * height * inner + (nb + 1) * side * side)
                + 4 * TBC * TB * height * side * max(1, len(grids) * 2)),
            cost_estimate=pl.CostEstimate(
                flops=2 * len(rights) * TB * height * inner * TBC * side,
                bytes_accessed=sum(g.size for g in rights) * 2,
                transcendentals=0,
            ),
            name=name,
        )(table, *near, *rights, *far)

    whole = jax.ShapeDtypeStruct((half, side, side), jnp.float32)
    spare = lax.select_n(col ^ row ^ 3, *a_got)
    tiles = spare[: na * side].reshape(na, side, side)
    upper, lower = (
        jnp.concatenate([g.reshape(na * low, side), spare[na * side :]])
        for g in (tiles[:, :low], tiles[:, low:])
    )
    upper, lower = flip(upper, 1), flip(lower, 2)

    own_table, pattern = right_tables(b_note[None])
    own_table = jnp.concatenate([left_table[:1], own_table, pattern, place])
    keep, give = call(own_blocks((0,)), "own_block", own_table, a_got, (b,), whole, side, ())
    a_got, b_x, b_y, b_note_x, b_note_y, keep, give = lax.optimization_barrier(
        (a_got, b_x, b_y, b_note_x, b_note_y, keep, give)
    )
    right_table, patterns = right_tables(jnp.stack([b_note_x, b_note_y]))
    table = jnp.concatenate([left_table[1:], right_table, pattern, place])
    keep, give = call(
        own_blocks((1, 2)), "near_blocks", table, (*a_got, keep, give), (b_x, b_y), whole, side, ()
    )
    upper, lower, keep, give = lax.optimization_barrier((upper, lower, keep, give))
    table = jnp.concatenate([right_table[1:], right_table[:1], patterns, place])
    part = jax.ShapeDtypeStruct((2, half, low, side), jnp.float32)
    part_keep, part_give = call(
        help_neighbours, "help_neighbours", table, (), (b_y, b_x), part, low, (2,), (upper, lower)
    )
    part_other = [swap_layers(part_give[q]) for q in range(2)]
    other = swap_layers(give)
    steps = half * low

    def encode(q):
        def kernel(keep, other, code):
            values = [keep[q, o] + other[o] for o in range(half)]
            tops = [jnp.max(jnp.abs(v), axis=0, keepdims=True) for v in values]
            top = jnp.maximum(jnp.concatenate(tops, axis=0), 1e-30)
            exponent = jnp.ceil(jnp.log2(top))
            scale = jnp.exp2(15.0 - exponent)
            for o, value in enumerate(values):
                value = jnp.clip(value * scale[o : o + 1, :], -32767.0, 32767.0)
                value = jnp.round(value).astype(jnp.int32)
                code[o * low : (o + 1) * low, :] = value.astype(jnp.int16)
            code[steps:, :] = exponent.astype(jnp.int32).astype(jnp.int16)

        return kernel

    def finish(mine, from_x, from_y, out, rounded, sems):
        codes = (from_x, from_y)
        scales = [jnp.exp2(c[steps:, :].astype(jnp.int32).astype(jnp.float32) - 15.0) for c in codes]
        copies = []
        for o in range(half):
            for q in range(2):
                at = (o, slice(q * low, (q + 1) * low), slice(None))
                part = codes[q][o * low : (o + 1) * low, :].astype(jnp.int32).astype(jnp.float32)
                rounded[at] = (mine[at] + part * scales[q][o : o + 1, :]).astype(rounded.dtype)
            if (o + 1) % (half // 4) == 0:
                done = slice(o + 1 - half // 4, o + 1)
                copies.append(
                    pltpu.make_async_copy(rounded.at[done], out.at[done], sems.at[len(copies)])
                )
                copies[-1].start()
        for c in copies:
            c.wait()

    code = jax.ShapeDtypeStruct((steps + half, side), jnp.int16)
    code_x, code_y = (
        pl.pallas_call(
            encode(q),
            in_specs=[vmem] * 2,
            out_specs=vmem,
            out_shape=code,
            compiler_params=pltpu.CompilerParams(vmem_limit_bytes=10 * 2**20),
            name=name,
        )(part_keep, part_other[q])
        for q, name in enumerate(("encode_x", "encode_y"))
    )
    from_x, from_y = flip(code_x, 1), flip(code_y, 2)
    mine = keep + other
    result = pl.pallas_call(
        finish,
        in_specs=[vmem] * 3,
        out_specs=hbm,
        out_shape=jax.ShapeDtypeStruct((half, side, side), jnp.bfloat16),
        scratch_shapes=[
            pltpu.VMEM((half, side, side), jnp.bfloat16),
            pltpu.SemaphoreType.DMA((4,)),
        ],
        name="finish",
        compiler_params=pltpu.CompilerParams(vmem_limit_bytes=10 * 2**20),
    )(mine, from_x, from_y)
    return result.reshape(1, 1, half, side, side)


def solution(mesh):
    if mesh.shape["row"] == 4 and mesh.shape["col"] == 4:
        body = planned_shards
    else:
        body = gathered_shards
    return jax.shard_map(
        body,
        mesh=mesh,
        in_specs=(
            P("row", "layer", "col", None, None, None),
            P("row", "layer", "col", None),
            P("row", "layer", "col"),
            P("layer", "row", "col", None, None, None),
            P("layer", "row", "col", None),
            P("layer", "row", "col"),
            P("row", "col", None),
        ),
        out_specs=P("row", "col", "layer", None, None),
        check_vma=False,
    )
```
